32 devices in a mesh: fsdp: 16 (over z, y, x), tensor: 2 (over core).
Axes of the slice: x: 2, y: 2, z: 4, core: 2. Of those that a mesh axis runs over, the one named last changes fastest.
Arguments:
- tokens: bfloat16 [50432, 768], P(('fsdp', 'tensor')), may hold values from -6 to 6
- w_qkv: bfloat16 [3, 768, 768], P(None, 'fsdp', 'tensor'), may hold values from -0.21875 to 0.21875
- b_qv: bfloat16 [2, 768], P(None, 'fsdp'), may hold values from -3 to 3
- w_out: bfloat16 [768, 768], P('tensor', 'fsdp'), may hold values from -1.75 to 1.75
- b_out: bfloat16 [768], P('fsdp'), may hold values from -2 to 2
- norm_gains: bfloat16 [2, 768], P(None, 'fsdp'), may hold values from 0.5 to 1.5
- norm_shifts: bfloat16 [2, 768], P(None, 'fsdp'), may hold values from -2 to 2
- w_fc1: bfloat16 [768, 3072], P('fsdp', 'tensor'), may hold values from -0.21875 to 0.21875
- b_fc1: bfloat16 [3072], P('fsdp'), may hold values from -3 to 3
- w_fc2: bfloat16 [3072, 768], P('tensor', 'fsdp'), may hold values from -0.109375 to 0.109375
- b_fc2: bfloat16 [768], P('fsdp'), may hold values from -2 to 2
- cotangent: bfloat16 [50432, 768], P(('fsdp', 'tensor')), may hold values from -6 to 6
Outputs:
- result: bfloat16 [50432, 768], P(('fsdp', 'tensor'))
- grad_tokens: bfloat16 [50432, 768], P(('fsdp', 'tensor'))
- grad_w_qkv: float32 [3, 768, 768], P(None, 'fsdp', 'tensor')
- grad_b_qv: float32 [2, 768], P(None, 'fsdp')
- grad_w_out: float32 [768, 768], P('tensor', 'fsdp')
- grad_b_out: float32 [768], P('fsdp')
- grad_norm_gains: float32 [2, 768], P(None, 'fsdp')
- grad_norm_shifts: float32 [2, 768], P(None, 'fsdp')
- grad_w_fc1: float32 [768, 3072], P('fsdp', 'tensor')
- grad_b_fc1: float32 [3072], P('fsdp')
- grad_w_fc2: float32 [3072, 768], P('tensor', 'fsdp')
- grad_b_fc2: float32 [768], P('fsdp')
The draws below stay inside these ranges and needn't reach their ends.
All inputs are finite; a program needn't handle non-finite values.
Results may differ from the reference program's by a relative error of at most 0.015.
Values may be sent and summed in bfloat16 or wider, within the bound.
A program may use at most 256 MiB of HBM per device.

```python
import jax
import jax.numpy as jnp
from jax import lax

D = 768
HEADS = 12
HDIM = 64
FF = 3072
SEQ = 197
IMG_DEV = 16
IMAGES = 256
TOKENS = 50432


def level_of(rng, dims, shards, least, top_value):
    level, own = 1.0, jax.random.fold_in(rng, 6)
    for position, shards_of in shards:
        steps = jnp.exp(jax.random.uniform(jax.random.fold_in(own, position), (shards_of,), jnp.float32, least / len(shards), top_value / len(shards)))
        level = level * jnp.repeat(steps, dims[position] // shards_of).reshape([-1 if axis == position else 1 for axis in range(len(dims))])
    return level


def normal_values(key, shape, scale, most, pieces=(), dtype=jnp.bfloat16):
    values = scale * jax.random.normal(key, shape, jnp.float32)
    if pieces:
        values = values * level_of(key, shape, pieces, -0.22, 0.18)
    return jnp.clip(values, -most, most).astype(dtype)


def setup_inputs(seed: int = 0) -> dict:
    arg_keys = jax.random.split(jax.random.key(seed), 13)
    tokens = normal_values(arg_keys[0], (TOKENS, D), 1.0, 6.0, ((0, 32),))
    w_qkv = normal_values(arg_keys[1], (3, D, D), D ** -0.5, 0.21875, ((1, 16), (2, 2)))
    b_qv = normal_values(arg_keys[2], (2, D), 0.5, 3.0, ((1, 16),))
    w_out = normal_values(arg_keys[3], (D, D), (D // 64) ** -0.5, 1.75, ((0, 2), (1, 16)))
    b_out = normal_values(arg_keys[4], (D,), 0.3, 2.0, ((0, 16),))
    norm_gains = jnp.clip(1.0 + 0.1 * jax.random.normal(arg_keys[5], (2, D), jnp.float32), 0.5, 1.5).astype(jnp.bfloat16)
    norm_shifts = normal_values(arg_keys[6], (2, D), 0.3, 2.0, ((1, 16),))
    w_fc1 = normal_values(arg_keys[7], (D, FF), D ** -0.5, 0.21875, ((0, 16), (1, 2)))
    b_fc1 = normal_values(arg_keys[8], (FF,), 0.5, 3.0, ((0, 16),))
    w_fc2 = normal_values(arg_keys[9], (FF, D), FF ** -0.5, 0.109375, ((0, 2), (1, 16)))
    b_fc2 = normal_values(arg_keys[10], (D,), 0.3, 2.0, ((0, 16),))
    cotangent = normal_values(arg_keys[11], (TOKENS, D), 1.0, 6.0, ((0, 32),))
    return {"tokens": tokens, "w_qkv": w_qkv, "b_qv": b_qv, "w_out": w_out, "b_out": b_out, "norm_gains": norm_gains, "norm_shifts": norm_shifts, "w_fc1": w_fc1, "b_fc1": b_fc1, "w_fc2": w_fc2, "b_fc2": b_fc2, "cotangent": cotangent}


@jax.custom_vjp
def low(v):
    return lax.optimization_barrier(v.astype(jnp.bfloat16)).astype(jnp.float32)

@jax.custom_vjp
def low_back(v):
    return v

def low_keep(v):
    return (low(v), None)

def low_pass(kept, grad):
    return (grad,)

def back_keep(v):
    return (v, None)

def back_low(kept, grad):
    return (low(grad),)
low.defvjp(low_keep, low_pass)
low_back.defvjp(back_keep, back_low)
EPS = 1e-06

def layer_norm(value, gain, shift):
    center = value - lax.optimization_barrier(jnp.mean(value, axis=-1, keepdims=True))
    spread = lax.optimization_barrier(jnp.mean(center * center, axis=-1, keepdims=True))
    return center * lax.rsqrt(spread + EPS) * gain + shift

def attend(triple):
    query, keys, values = triple
    highest = lax.Precision.HIGHEST
    scores = jnp.einsum('bshd,bkhd->bhsk', query, keys, precision=highest) * HDIM ** (-0.5)
    scores = low_back(scores)
    probs = low(jax.nn.softmax(scores, axis=-1))
    return jnp.einsum('bhsk,bkhd->bshd', probs, values, precision=highest)

def forward(resid, w_qkv, b_qv, w_out, b_out, norm_gains, norm_shifts, w_fc1, b_fc1, w_fc2, b_fc2):
    highest = lax.Precision.HIGHEST
    normed1 = low(layer_norm(resid, norm_gains[0], norm_shifts[0]))
    query = low(low_back(jnp.dot(normed1, w_qkv[0], precision=highest) + b_qv[0]))
    keys = low(low_back(jnp.dot(normed1, w_qkv[1], precision=highest)))
    values = low(low_back(jnp.dot(normed1, w_qkv[2], precision=highest) + b_qv[1]))
    blocks = IMAGES // IMG_DEV
    shaped = [t.reshape(blocks, IMG_DEV, SEQ, HEADS, HDIM) for t in (query, keys, values)]
    mixed = lax.map(jax.checkpoint(attend), (shaped[0], shaped[1], shaped[2]))
    attended = low(low_back(mixed.reshape(TOKENS, D)))
    branch1 = low_back(jnp.dot(attended, w_out, precision=highest) + b_out)
    mid = resid + branch1
    normed2 = low(layer_norm(mid, norm_gains[1], norm_shifts[1]))
    hidden = low_back(jnp.dot(normed2, w_fc1, precision=highest) + b_fc1)
    activ = low(jax.nn.gelu(hidden, approximate=False))
    branch2 = low_back(jnp.dot(activ, w_fc2, precision=highest) + b_fc2)
    return mid + branch2

def reference(tokens, w_qkv, b_qv, w_out, b_out, norm_gains, norm_shifts, w_fc1, b_fc1, w_fc2, b_fc2, cotangent):
    inputs = [a.astype(jnp.float32) for a in (tokens, w_qkv, b_qv, w_out, b_out, norm_gains, norm_shifts, w_fc1, b_fc1, w_fc2, b_fc2)]
    output, pullback = jax.vjp(forward, *inputs)
    grads = pullback(cotangent.astype(jnp.float32))
    return (output.astype(jnp.bfloat16), grads[0].astype(jnp.bfloat16), grads[1], grads[2], grads[3], grads[4], grads[5], grads[6], grads[7], grads[8], grads[9], grads[10])
```

```python
import jax
import jax.numpy as jnp
from jax import lax
from jax.experimental import pallas as pl
from jax.experimental.pallas import tpu as pltpu
from jax.sharding import PartitionSpec as P

HDIM = 64
SEQ = 197
PAD = 208
EPS = 1e-06
LANES = 128
F32 = jnp.float32
BF16 = jnp.bfloat16

NT = (((1,), (1,)), ((), ()))
TN = (((0,), (0,)), ((), ()))
NN = (((1,), (0,)), ((), ()))


def mm(a, b, dims):
    return lax.dot_general(a, b, dims, preferred_element_type=F32)


def pair_masks():
    lane = lax.broadcasted_iota(jnp.int32, (1, LANES), 1)
    low = lane < HDIM
    scale = HDIM ** (-0.5)
    picks = (
        jnp.where(low, 1.0, 0.0).astype(BF16),
        jnp.where(low, 0.0, 1.0).astype(BF16),
    )
    scaled = (
        jnp.where(low, scale, 0.0).astype(BF16),
        jnp.where(low, 0.0, scale).astype(BF16),
    )
    return low, picks, scaled


def attend_kernel(own_ref, other_ref, att_ref, lse_ref):
    cols = own_ref.shape[2] // 3
    low, _, scaled = pair_masks()
    real = lax.broadcasted_iota(jnp.int32, (PAD, 1), 0) < SEQ
    lse_ref[...] = jnp.zeros_like(lse_ref)
    head = 0
    for side, ref in enumerate((own_ref, other_ref)):
        for start in range(0, cols, LANES):
            query = ref[0, :, start : start + LANES]
            keys = ref[0, :, cols + start : cols + start + LANES]
            values = ref[0, :, 2 * cols + start : 2 * cols + start + LANES]
            mixed = []
            for part in range(2):
                scores = mm(keys * scaled[part], query, NT)
                scores = jnp.where(real, scores, -1e30)
                top = jnp.max(scores, axis=0, keepdims=True)
                expd = jnp.exp(scores - top)
                total = jnp.sum(expd, axis=0, keepdims=True)
                probs = (expd * (1.0 / total)).astype(BF16)
                lse_ref[0, head : head + 1, :] = top + jnp.log(total)
                mixed.append(mm(probs, values, TN))
                head += 1
            at = side * cols + start
            att_ref[0, :, at : at + LANES] = jnp.where(low, mixed[0], mixed[1]).astype(BF16)


def attend_back_kernel(own_ref, other_ref, grad_ref, lse_ref, gown_ref, gother_ref):
    cols = own_ref.shape[2] // 3
    low, picks, scaled = pair_masks()
    scale = HDIM ** (-0.5)
    real = lax.broadcasted_iota(jnp.int32, (PAD, 1), 0) < SEQ
    head = 0
    for side, (ref, out) in enumerate(((own_ref, gown_ref), (other_ref, gother_ref))):
        for start in range(0, cols, LANES):
            query = ref[0, :, start : start + LANES]
            keys = ref[0, :, cols + start : cols + start + LANES]
            values = ref[0, :, 2 * cols + start : 2 * cols + start + LANES]
            at = side * cols + start
            grad = grad_ref[0, :, at : at + LANES]
            gq, gk, gv = [], [], []
            for part in range(2):
                keys_part = keys * scaled[part]
                scores = mm(keys_part, query, NT)
                probs = jnp.where(real, jnp.exp(scores - lse_ref[0, head : head + 1, :]), 0.0)
                gprobs = mm(values * picks[part], grad, NT)
                inner = jnp.sum(probs * gprobs, axis=0, keepdims=True)
                gscores = (probs * (gprobs - inner)).astype(BF16)
                gq.append(mm(gscores, keys_part, TN))
                gk.append(mm(gscores, query, NN))
                gv.append(mm(probs.astype(BF16), grad, NN))
                head += 1
            out[0, :, start : start + LANES] = (gq[0] + gq[1]).astype(BF16)
            out[0, :, cols + start : cols + start + LANES] = (
                jnp.where(low, gk[0], gk[1]) * scale
            ).astype(BF16)
            out[0, :, 2 * cols + start : 2 * cols + start + LANES] = jnp.where(
                low, gv[0], gv[1]
            ).astype(BF16)


def image_block(rows, cols):
    return pl.BlockSpec((1, rows, cols), lambda i: (i, 0, 0))


def attend(own, other):
    images, _, width = own.shape
    cols = width // 3
    heads = 2 * cols // HDIM
    lse_rows = -(-heads // 8) * 8
    return pl.pallas_call(
        attend_kernel,
        grid=(images,),
        in_specs=[image_block(PAD, width)] * 2,
        out_specs=[image_block(PAD, 2 * cols), image_block(lse_rows, PAD)],
        out_shape=[
            jax.ShapeDtypeStruct((images, PAD, 2 * cols), BF16),
            jax.ShapeDtypeStruct((images, lse_rows, PAD), F32),
        ],
        compiler_params=pltpu.CompilerParams(vmem_limit_bytes=32 * 1024 * 1024),
        cost_estimate=pl.CostEstimate(
            flops=images * heads * PAD * PAD * 64 * 4 * 4,
            bytes_accessed=images * PAD * 8 * cols * 2,
            transcendentals=images * heads * PAD * PAD,
        ),
    )(own, other)


def attend_back(own, other, grad, lse):
    images, _, width = own.shape
    cols = width // 3
    heads = 2 * cols // HDIM
    return pl.pallas_call(
        attend_back_kernel,
        grid=(images,),
        in_specs=[image_block(PAD, width)] * 2
        + [image_block(PAD, 2 * cols), image_block(lse.shape[1], PAD)],
        out_specs=[image_block(PAD, width)] * 2,
        out_shape=[jax.ShapeDtypeStruct((images, PAD, width), BF16)] * 2,
        compiler_params=pltpu.CompilerParams(vmem_limit_bytes=32 * 1024 * 1024),
        cost_estimate=pl.CostEstimate(
            flops=images * heads * PAD * PAD * 64 * 10 * 4,
            bytes_accessed=images * PAD * 14 * cols * 2,
            transcendentals=images * heads * PAD * PAD,
        ),
    )(own, other, grad, lse)


def normalize(value):
    center = value - jnp.mean(value, axis=-1, keepdims=True)
    spread = jnp.mean(center * center, axis=-1, keepdims=True)
    inv = lax.rsqrt(spread + EPS)
    return center * inv, inv


def norm_grad(grad, gain, xhat, inv):
    dx = grad * gain
    return inv * (
        dx - jnp.mean(dx, axis=-1, keepdims=True) - xhat * jnp.mean(dx * xhat, axis=-1, keepdims=True)
    )


def swap(value):
    return lax.ppermute(value, "tensor", [(0, 1), (1, 0)])


def body(
    tokens,
    w_qkv,
    b_qv,
    w_out,
    b_out,
    norm_gains,
    norm_shifts,
    w_fc1,
    b_fc1,
    w_fc2,
    b_fc2,
    cotangent,
):
    parts = lax.axis_size("tensor")
    assert parts == 2
    place = lax.axis_index("tensor")
    rows, width = tokens.shape
    depth = w_qkv.shape[1]
    cols = w_qkv.shape[2]
    units = w_fc1.shape[1]
    images = rows // SEQ
    per_row = b_fc1.shape[0] // depth

    small_in = jnp.concatenate(
        [norm_gains, norm_shifts, b_qv, b_out[None], b_fc2[None], b_fc1.reshape(depth, per_row).T],
        axis=0,
    ).T
    count = small_in.shape[1]
    small_in = jnp.pad(small_in, ((0, 0), (0, LANES - count)))
    panel = jnp.concatenate([w_qkv[0], w_qkv[1], w_qkv[2], w_out.T, small_in], axis=1)
    panel = lax.all_gather(panel, "fsdp", axis=0, tiled=True)
    mlp_own = lax.all_gather(
        jnp.concatenate([w_fc1, w_fc2.T], axis=1), "fsdp", axis=0, tiled=True
    )
    attn_cols = 4 * cols
    qkv_w = [panel[:, : 3 * cols]]
    attn_other = swap(panel[:, :attn_cols])
    qkv_w.append(attn_other[:, : 3 * cols])
    mlp_other = swap(mlp_own)
    fc1 = [mlp_own[:, :units], mlp_other[:, :units]]
    fc2 = [mlp_own[:, units:], mlp_other[:, units:]]
    out_t = jnp.concatenate([panel[:, 3 * cols : attn_cols], attn_other[:, 3 * cols :]], axis=1)
    small_full = panel[:, attn_cols : attn_cols + count].astype(F32).T
    gains, shifts, bias_qv = small_full[0:2], small_full[2:4], small_full[4:6]
    bias_out, bias_fc2 = small_full[6], small_full[7]
    bias_fc1 = small_full[8 : 8 + per_row].T.reshape(-1)

    def halves(vector, size):
        return [
            lax.dynamic_slice_in_dim(vector, place * size, size, 0),
            lax.dynamic_slice_in_dim(vector, (1 - place) * size, size, 0),
        ]

    def joined(own, other):
        return jnp.where(
            place == 0, jnp.concatenate([own, other]), jnp.concatenate([other, own])
        )

    bias_q, bias_v = halves(bias_qv[0], cols), halves(bias_qv[1], cols)
    bias_hidden = halves(bias_fc1, units)

    def padded(value):
        return jnp.pad(
            value.reshape(images, SEQ, width), ((0, 0), (0, PAD - SEQ), (0, 0))
        ).reshape(images * PAD, width)

    def cut(value):
        return value.reshape(images, PAD, width)[:, :SEQ].reshape(rows, width)

    resid = padded(tokens).astype(F32)
    cot = padded(cotangent)
    xhat1, inv1 = normalize(resid)
    normed1 = (xhat1 * gains[0] + shifts[0]).astype(BF16)
    qkv = []
    for p in range(2):
        bias = jnp.concatenate([bias_q[p], jnp.zeros((cols,), F32), bias_v[p]])
        qkv.append(
            (mm(normed1, qkv_w[p], NN) + bias).astype(BF16).reshape(images, PAD, 3 * cols)
        )
    attended, lse = attend(qkv[0], qkv[1])
    attended = attended.reshape(images * PAD, 2 * cols)
    mid = resid + (mm(attended, out_t, NT) + bias_out)
    xhat2, inv2 = normalize(mid)
    normed2 = (xhat2 * gains[1] + shifts[1]).astype(BF16)
    activ, slope = [], []
    for p in range(2):
        hidden = mm(normed2, fc1[p], NN) + bias_hidden[p]
        cdf = 0.5 * (1.0 + lax.erf(hidden * (2.0**-0.5)))
        pdf = jnp.exp(-0.5 * hidden * hidden) * 0.3989422804014327
        activ.append((hidden * cdf).astype(BF16))
        slope.append((cdf + hidden * pdf).astype(BF16))
    result = (mid + (mm(activ[0], fc2[0], NT) + mm(activ[1], fc2[1], NT) + bias_fc2)).astype(BF16)

    grad_fc2 = [mm(cot, activ[p], TN) for p in range(2)]
    total_fc2 = (grad_fc2[0] + swap(grad_fc2[1].astype(BF16)).astype(F32)).astype(BF16)
    grad_hidden = [
        (mm(cot, fc2[p], NN) * slope[p].astype(F32)).astype(BF16) for p in range(2)
    ]
    grad_normed2 = mm(grad_hidden[0], fc1[0], NT) + mm(grad_hidden[1], fc1[1], NT)
    grad_fc1 = [mm(normed2, grad_hidden[p], TN) for p in range(2)]
    total_fc1 = (grad_fc1[0] + swap(grad_fc1[1].astype(BF16)).astype(F32)).astype(BF16)
    sent_mlp = lax.psum_scatter(
        jnp.concatenate([total_fc1, total_fc2], axis=1), "fsdp", scatter_dimension=0, tiled=True
    )
    hidden_sums = [jnp.sum(grad_hidden[p].astype(F32), axis=0) for p in range(2)]

    upstream = cot.astype(F32)
    grad_mid = upstream + norm_grad(grad_normed2, gains[1], xhat2, inv2)
    grad_branch = grad_mid.astype(BF16)
    grad_attended = mm(grad_branch, out_t, NN).astype(BF16)
    grad_out_t = mm(grad_branch, attended, TN)
    grad_qkv = attend_back(
        qkv[0], qkv[1], grad_attended.reshape(images, PAD, 2 * cols), lse
    )
    grad_qkv = [g.reshape(images * PAD, 3 * cols) for g in grad_qkv]
    grad_qkv_w = [mm(normed1, g, TN) for g in grad_qkv]
    qkv_sums = [jnp.sum(g.astype(F32), axis=0) for g in grad_qkv]
    grad_normed1 = mm(grad_qkv[0], qkv_w[0], NT) + mm(grad_qkv[1], qkv_w[1], NT)
    grad_tokens = (grad_mid + norm_grad(grad_normed1, gains[0], xhat1, inv1)).astype(BF16)

    small = jnp.concatenate(
        [
            jnp.stack(
                [
                    jnp.sum(grad_normed1 * xhat1, axis=0),
                    jnp.sum(grad_normed2 * xhat2, axis=0),
                    jnp.sum(grad_normed1, axis=0),
                    jnp.sum(grad_normed2, axis=0),
                    joined(qkv_sums[0][:cols], qkv_sums[1][:cols]),
                    joined(qkv_sums[0][2 * cols :], qkv_sums[1][2 * cols :]),
                    jnp.sum(grad_branch.astype(F32), axis=0),
                    jnp.sum(upstream, axis=0),
                ]
            ),
            joined(hidden_sums[0], hidden_sums[1]).reshape(width, per_row).T,
        ],
        axis=0,
    ).T
    small = jnp.pad(small, ((0, 0), (0, LANES - count))).astype(BF16)
    away = jnp.concatenate(
        [grad_qkv_w[1].astype(BF16), grad_out_t[:, cols:].astype(BF16), small], axis=1
    )
    home = jnp.concatenate([grad_qkv_w[0], grad_out_t[:, :cols], small.astype(F32)], axis=1)
    total = (home + swap(away).astype(F32)).astype(BF16)
    sent = lax.psum_scatter(total, "fsdp", scatter_dimension=0, tiled=True).astype(F32)
    sent_qkv = jnp.stack([sent[:, i * cols : (i + 1) * cols] for i in range(3)])
    sent_small = sent[:, attn_cols : attn_cols + count].T
    return (
        cut(result),
        cut(grad_tokens),
        sent_qkv,
        sent_small[4:6],
        sent[:, 3 * cols : attn_cols].T,
        sent_small[6],
        sent_small[0:2],
        sent_small[2:4],
        sent_mlp[:, :units].astype(F32),
        sent_small[8 : 8 + per_row].T.reshape(-1),
        sent_mlp[:, units:].astype(F32).T,
        sent_small[7],
    )


def solution(mesh):
    both = P(("fsdp", "tensor"), None)
    placed = (
        both,
        P(None, "fsdp", "tensor"),
        P(None, "fsdp"),
        P("tensor", "fsdp"),
        P("fsdp"),
        P(None, "fsdp"),
        P(None, "fsdp"),
        P("fsdp", "tensor"),
        P("fsdp"),
        P("tensor", "fsdp"),
        P("fsdp"),
        both,
    )
    return jax.shard_map(
        body,
        mesh=mesh,
        in_specs=placed,
        out_specs=(
            both,
            both,
            P(None, "fsdp", "tensor"),
            P(None, "fsdp"),
            P("tensor", "fsdp"),
            P("fsdp"),
            P(None, "fsdp"),
            P(None, "fsdp"),
            P("fsdp", "tensor"),
            P("fsdp"),
            P("tensor", "fsdp"),
            P("fsdp"),
        ),
        check_vma=False,
    )
```
